512 devices in a mesh: blk: 256 (over z, x_lo, y, core), pair: 2 (over x_hi).
Axes of the slice: x: 4 (x_hi: 2, x_lo: 2; x = x_hi * 2 + x_lo), y: 4, z: 16, core: 2. Of those that a mesh axis runs over, the one named last changes fastest.
Arguments:
- tokens: bfloat16 [256, 8192], P('blk', 'pair'), may hold values from -6 to 6
- out_cot: bfloat16 [256, 8192], P('blk', 'pair'), may hold values from -3 to 3
- gate_rows: bfloat16 [24576, 8192], P('blk', 'pair'), may hold values from -0.0625 to 0.0625
- up_rows: bfloat16 [24576, 8192], P('blk', 'pair'), may hold values from -0.0625 to 0.0625
- down_rows: bfloat16 [24576, 8192], P('blk', 'pair'), may hold values from -0.0390625 to 0.0390625
Outputs:
- input_grads: bfloat16 [256, 8192], P('blk', 'pair')
- gate_grads: bfloat16 [24576, 8192], P('blk', 'pair')
- up_grads: bfloat16 [24576, 8192], P('blk', 'pair')
- down_grads: bfloat16 [24576, 8192], P('blk', 'pair')
The draws below stay inside these ranges and needn't reach their ends.
All inputs are finite; a program needn't handle non-finite values.
Results may differ from the reference program's by a relative error of at most 0.005.
Values may be sent and summed in bfloat16 or wider, within the bound.
A program may use at most 64 MiB of HBM per device.

```python
import jax
import jax.numpy as jnp
from jax import lax

D = 8192
UNITS_DEV = 96
FF = 24576
TOKENS = 256
N_BLK = 256


def level_of(rng, extent, shards, smallest, largest):
    loudness, own = 1.0, jax.random.fold_in(rng, 6)
    for dim, blocks in shards:
        steps = jnp.exp(jax.random.uniform(jax.random.fold_in(own, dim), (blocks,), jnp.float32, smallest / len(shards), largest / len(shards)))
        loudness = loudness * jnp.repeat(steps, extent[dim] // blocks).reshape([-1 if axis == dim else 1 for axis in range(len(extent))])
    return loudness


def gaussian(own_key, extent, width, most, split=(), held_as=jnp.bfloat16):
    array = jax.random.normal(own_key, extent, jnp.float32) * width
    if len(split) > 0:
        array = level_of(own_key, extent, split, -0.22, 0.18) * array
    return jnp.clip(array, min=-most, max=most).astype(held_as)


def setup_inputs(seed: int = 0) -> dict:
    key_list = jax.random.split(jax.random.key(seed), 6)
    return {
        "tokens": gaussian(key_list[0], (TOKENS, D), 1.0, 6.0, ((0, 256), (1, 2))),
        "out_cot": gaussian(key_list[1], (TOKENS, D), 0.5, 3.0, ((0, 256), (1, 2))),
        "gate_rows": gaussian(key_list[2], (FF, D), D ** -0.5, 0.0625, ((0, 256), (1, 2))),
        "up_rows": gaussian(key_list[3], (FF, D), D ** -0.5, 0.0625, ((0, 256), (1, 2))),
        "down_rows": gaussian(key_list[4], (FF, D), FF ** -0.5, 0.0390625, ((0, 256), (1, 2))),
    }


def reference(tokens, out_cot, gate_rows, up_rows, down_rows):
    dmodel = tokens.shape[1]
    stacked = tuple(weights.reshape(N_BLK, UNITS_DEV, dmodel) for weights in (gate_rows, up_rows, down_rows))

    def panel_step(input_sum, panel):
        w_gate, w_up, w_down = panel
        gate_act = jnp.dot(tokens, w_gate.T, preferred_element_type=jnp.float32)
        up_act = jnp.dot(tokens, w_up.T, preferred_element_type=jnp.float32)
        hid_grad = jnp.dot(out_cot, w_down.T, preferred_element_type=jnp.float32)
        sigmoid_gate = jax.nn.sigmoid(gate_act)
        silu_gate = gate_act * sigmoid_gate
        hidden = (silu_gate * up_act).astype(jnp.bfloat16)
        up_grad = (hid_grad * silu_gate).astype(jnp.bfloat16)
        gate_grad = (hid_grad * up_act * sigmoid_gate * (1.0 + gate_act * (1.0 - sigmoid_gate))).astype(jnp.bfloat16)
        input_sum = input_sum + jnp.dot(gate_grad, w_gate, preferred_element_type=jnp.float32) + jnp.dot(up_grad, w_up, preferred_element_type=jnp.float32)
        gate_part = jnp.dot(gate_grad.T, tokens, preferred_element_type=jnp.float32).astype(jnp.bfloat16)
        up_part = jnp.dot(up_grad.T, tokens, preferred_element_type=jnp.float32).astype(jnp.bfloat16)
        down_part = jnp.dot(hidden.T, out_cot, preferred_element_type=jnp.float32).astype(jnp.bfloat16)
        return input_sum, (gate_part, up_part, down_part)

    start_sum = jnp.zeros((tokens.shape[0], dmodel), jnp.float32)
    input_sum, parts = lax.scan(panel_step, start_sum, stacked)
    input_grads = input_sum.astype(jnp.bfloat16)
    gate_grads = parts[0].reshape(N_BLK * UNITS_DEV, dmodel)
    up_grads = parts[1].reshape(N_BLK * UNITS_DEV, dmodel)
    down_grads = parts[2].reshape(N_BLK * UNITS_DEV, dmodel)
    return input_grads, gate_grads, up_grads, down_grads
```

```python
import functools

import jax
import jax.numpy as jnp
from jax import lax
from jax.experimental import pallas as pl
from jax.experimental.pallas import tpu as pltpu
from jax.sharding import PartitionSpec as P

MESH = pl.DeviceIdType.MESH
F32, BF16 = jnp.float32, jnp.bfloat16
NZ, NPLANE = 16, 16
UNITS, WIDTH, HALF = 96, 4096, 2048
ROWS = NZ * NPLANE
CW, NC = 512, 4


def dot(left, right, dims):
    return lax.dot_general(left, right, (dims, ((), ())), preferred_element_type=F32)


def kernel(
    tok_ref, cot_ref, gate_ref, up_ref, down_ref,
    in_out, gate_out, up_out, down_out,
    row, msg, plane, planef, g, wgu, wd, pre, pre_send, pre_recv, act, act_t, hid,
    mine, sib_send, sib_recv, rs_send, rs_recv, fin, fin_recv, line, ogu, od,
    w_sem, p_ss, p_rs, z_ss, z_rs, s_ss, s_rs, x_ss, x_rs, t_ss, t_rs, r_ss, r_rs, f_ss, f_rs, o_sem,
):
    blk, pair = lax.axis_index("blk"), lax.axis_index("pair")
    z, me, core = blk // NPLANE, lax.rem(blk, NPLANE), lax.rem(blk, 2)

    def at(zz, pp):
        return (zz * NPLANE + pp, pair)

    z_next = (at(lax.rem(z + 1, NZ), me), at(lax.rem(z + NZ - 1, NZ), me))
    sibling = at(z, me + 1 - 2 * core)
    partner = (blk, 1 - pair)
    spots = [lax.rem(me + k, NPLANE) for k in range(NPLANE)]

    loads = [
        pltpu.make_async_copy(gate_ref, wgu.at[pl.ds(0, UNITS)], w_sem.at[0]),
        pltpu.make_async_copy(up_ref, wgu.at[pl.ds(UNITS, UNITS)], w_sem.at[1]),
        pltpu.make_async_copy(down_ref, wd, w_sem.at[2]),
    ]
    for load in loads:
        load.start()

    barrier = pltpu.get_barrier_semaphore()
    peers = [at(z, spot) for spot in spots[1:]] + list(z_next) + [partner]
    for peer in peers:
        pl.semaphore_signal(barrier, inc=1, device_id=peer, device_id_type=MESH)

    sent = []

    def send(src, dst, ss, rs, to):
        copy = pltpu.make_async_remote_copy(
            src_ref=src, dst_ref=dst, send_sem=ss, recv_sem=rs, device_id=to, device_id_type=MESH
        )
        copy.start()
        sent.append(copy)
        return copy

    for t, ref in enumerate((tok_ref, cot_ref)):
        own = ref[...].astype(F32)
        for s in range(32):
            row[t, s : s + 1, :] = own[:, s * 128 : (s + 1) * 128]
        for h in range(2):
            msg[h, t] = row[t, h * 16 : (h + 1) * 16, :].astype(BF16)
    pl.semaphore_wait(barrier, len(peers))

    swaps = [
        send(msg.at[lax.rem(spots[k], 2)], plane.at[me], p_ss.at[k], p_rs.at[k], at(z, spots[k]))
        for k in range(1, NPLANE)
    ]
    plane[pl.ds(me, 1)] = msg[pl.ds(core, 1)]
    for swap in swaps:
        swap.wait_recv()
    for t in range(2):
        planef[t] = plane[:, t].astype(F32)
        for s in range(16):
            g[core, 0, s, t] = planef[t, :, s, :].astype(BF16)

    def block(slot, n):
        return g.at[core, slot, pl.ds(8 * n, 8)]

    hops = {}

    def hop(d, k, n):
        if k == 8 and n != d:
            return
        src = (NZ + 1 - k) % NZ if d == 0 else k - 1
        dst = NZ - k if d == 0 else k
        hops[d, k, n] = send(block(src, n), block(dst, n), z_ss.at[d, k - 1, n], z_rs.at[d, k - 1, n], z_next[d])

    hands = []

    def hand(slot):
        ref = g.at[core, slot]
        hands.append(send(ref, ref, s_ss.at[slot], s_rs.at[slot], sibling))

    for n in range(2):
        for d in range(2):
            hop(d, 1, n)
    hand(0)
    for k in range(1, 8):
        for n in range(2):
            for d in range(2):
                hops[d, k, n].wait_recv()
                hop(d, k + 1, n)
        hand(NZ - k)
        hand(k)
    hops[0, 8, 0].wait_recv()
    hops[1, 8, 1].wait_recv()
    hand(8)
    for load in loads:
        load.wait()
    for copy in hands:
        copy.wait_recv()

    def rows_of(h, chunk, t):
        return jnp.concatenate([g[h, :, chunk * 4 + j, t].reshape(ROWS, 128) for j in range(4)], axis=1)

    for h in range(2):
        for chunk in range(NC):
            cols = slice(h * HALF + chunk * CW, h * HALF + (chunk + 1) * CW)
            gu = dot(wgu[:, cols], rows_of(h, chunk, 0), ((1,), (1,)))
            dn = dot(wd[:, cols], rows_of(h, chunk, 1), ((1,), (1,)))
            if h == 0 and chunk == 0:
                pre[: 2 * UNITS], pre[2 * UNITS :] = gu, dn
            else:
                pre[: 2 * UNITS] += gu
                pre[2 * UNITS :] += dn
    pre_send[...] = pre[...].astype(BF16)
    send(pre_send, pre_recv, x_ss, x_rs, partner).wait_recv()

    def total(i):
        part = slice(i * UNITS, (i + 1) * UNITS)
        return pre[part] + pre_recv[part].astype(F32)

    gate_act, up_act, hid_grad = total(0), total(1), total(2)
    sigmoid_gate = jax.nn.sigmoid(gate_act)
    silu_gate = gate_act * sigmoid_gate
    hid[...] = (silu_gate * up_act).astype(BF16)
    up_grad = hid_grad * silu_gate
    gate_grad = hid_grad * up_act * sigmoid_gate * (1.0 + gate_act * (1.0 - sigmoid_gate))
    act[:UNITS] = gate_grad.astype(BF16)
    act[UNITS:] = up_grad.astype(BF16)
    act_t[...] = act[...].astype(F32).T.astype(BF16)

    def columns(h, chunk):
        return pl.ds(pl.multiple_of(h * HALF + chunk * CW, CW), CW)

    sides = []
    for chunk in range(NC):
        part = dot(act_t[...], wgu[:, columns(1 - core, chunk)], ((1,), (0,)))
        sib_send[chunk] = part.astype(BF16)
        sides.append(send(sib_send.at[chunk], sib_recv.at[chunk], t_ss.at[chunk], t_rs.at[chunk], sibling))
    for chunk in range(NC):
        mine[chunk] = dot(act_t[...], wgu[:, columns(core, chunk)], ((1,), (0,)))
    for side in sides:
        side.wait_recv()

    def own_part(slot, n):
        here = slice(slot * 16, (slot + 1) * 16)
        return jnp.concatenate(
            [mine[c, here, :] + sib_recv[c, here, :].astype(F32) for c in (2 * n, 2 * n + 1)], axis=1
        )

    outs = []

    def weight_chunk(h, chunk):
        i = h * NC + chunk
        cols = slice(i * CW, (i + 1) * CW)
        ogu[:, cols] = dot(act[...], rows_of(h, chunk, 0), ((1,), (0,))).astype(BF16)
        od[:, cols] = dot(hid[...], rows_of(h, chunk, 1), ((1,), (0,))).astype(BF16)
        for j, (src, dst) in enumerate(
            (
                (ogu.at[pl.ds(0, UNITS), cols], gate_out.at[:, cols]),
                (ogu.at[pl.ds(UNITS, UNITS), cols], up_out.at[:, cols]),
                (od.at[:, cols], down_out.at[:, cols]),
            )
        ):
            copy = pltpu.make_async_copy(src, dst, o_sem.at[i, j])
            copy.start()
            outs.append(copy)

    sums = {}
    for k in range(1, 9):
        for n in range(2):
            for d in range(2):
                first = 1 if n == d else 2
                if k < first:
                    continue
                slot = 9 - k if d == 0 else 7 + k
                value = own_part(slot, n)
                if k > first:
                    sums[d, k - 1, n].wait_recv()
                    value = value + rs_recv[d, k - 2, n]
                rs_send[d, k - 1, n] = value
                sums[d, k, n] = send(
                    rs_send.at[d, k - 1, n], rs_recv.at[d, k - 1, n], r_ss.at[d, k - 1, n], r_rs.at[d, k - 1, n], z_next[d]
                )
        weight_chunk((k - 1) // NC, (k - 1) % NC)
    for n in range(2):
        value = own_part(0, n)
        for d in range(2):
            sums[d, 8, n].wait_recv()
            value = value + rs_recv[d, 7, n]
        for s in range(8):
            fin[:, n * 8 + s, :] = value[:, s * 128 : (s + 1) * 128]

    last = [
        send(fin.at[spots[k]], fin_recv.at[k], f_ss.at[k], f_rs.at[k], at(z, spots[k])) for k in range(1, NPLANE)
    ]
    halves = [fin[pl.ds(me, 1)].reshape(16, 128), None]
    for k in range(1, NPLANE):
        last[k - 1].wait_recv()
        halves[k % 2] = fin_recv[k] if halves[k % 2] is None else halves[k % 2] + fin_recv[k]
    for i, value in enumerate(halves):
        h = core if i == 0 else 1 - core
        for s in range(16):
            line[0:1, pl.ds(pl.multiple_of(h * HALF + s * 128, 128), 128)] = value[s : s + 1, :]
    in_out[...] = line[...].astype(BF16)
    for copy in sent:
        copy.wait_send()
    for copy in outs:
        copy.wait()


def local(tokens, out_cot, gate_rows, up_rows, down_rows):
    vmem, hbm = pl.BlockSpec(memory_space=pltpu.VMEM), pl.BlockSpec(memory_space=pl.ANY)
    dma = pltpu.SemaphoreType.DMA
    grads = jax.ShapeDtypeStruct((UNITS, WIDTH), BF16)
    return pl.pallas_call(
        kernel,
        out_shape=(jax.ShapeDtypeStruct((1, WIDTH), BF16), grads, grads, grads),
        in_specs=[vmem, vmem, hbm, hbm, hbm],
        out_specs=(vmem, hbm, hbm, hbm),
        scratch_shapes=[
            pltpu.VMEM((2, 32, 128), F32),
            pltpu.VMEM((2, 2, 16, 128), BF16),
            pltpu.VMEM((NPLANE, 2, 16, 128), BF16),
            pltpu.VMEM((2, NPLANE, 16, 128), F32),
            pltpu.VMEM((2, NZ, 16, 2, NPLANE, 128), BF16),
            pltpu.VMEM((2 * UNITS, WIDTH), BF16),
            pltpu.VMEM((UNITS, WIDTH), BF16),
            pltpu.VMEM((3 * UNITS, ROWS), F32),
            pltpu.VMEM((3 * UNITS, ROWS), BF16),
            pltpu.VMEM((3 * UNITS, ROWS), BF16),
            pltpu.VMEM((2 * UNITS, ROWS), BF16),
            pltpu.VMEM((ROWS, 2 * UNITS), BF16),
            pltpu.VMEM((UNITS, ROWS), BF16),
            pltpu.VMEM((NC, ROWS, CW), F32),
            pltpu.VMEM((NC, ROWS, CW), BF16),
            pltpu.VMEM((NC, ROWS, CW), BF16),
            pltpu.VMEM((2, 8, 2, 16, 1024), F32),
            pltpu.VMEM((2, 8, 2, 16, 1024), F32),
            pltpu.VMEM((NPLANE, 16, 128), F32),
            pltpu.VMEM((NPLANE, 16, 128), F32),
            pltpu.VMEM((1, WIDTH), F32),
            pltpu.VMEM((2 * UNITS, WIDTH), BF16),
            pltpu.VMEM((UNITS, WIDTH), BF16),
            dma((3,)),
            dma((NPLANE,)), dma((NPLANE,)),
            dma((2, 8, 2)), dma((2, 8, 2)),
            dma((NZ,)), dma((NZ,)),
            dma, dma,
            dma((NC,)), dma((NC,)),
            dma((2, 8, 2)), dma((2, 8, 2)),
            dma((NPLANE,)), dma((NPLANE,)),
            dma((2 * NC, 3)),
        ],
        compiler_params=pltpu.CompilerParams(
            collective_id=0, has_side_effects=True, vmem_limit_bytes=60 * 1024 * 1024
        ),
        name="swiglu_backward",
    )(tokens, out_cot, gate_rows, up_rows, down_rows)


def solution(mesh):
    specs = (P("blk", "pair"),) * 5
    return jax.shard_map(local, mesh=mesh, in_specs=specs, out_specs=specs[:4], check_vma=False)
```

```python
import functools

import jax
import jax.numpy as jnp
from jax import lax
from jax.experimental import pallas as pl
from jax.experimental.pallas import tpu as pltpu
from jax.sharding import PartitionSpec as P

MESH = pl.DeviceIdType.MESH
F32, BF16 = jnp.float32, jnp.bfloat16
NZ, NPLANE = 16, 16
UNITS, WIDTH, HALF = 96, 4096, 2048
ROWS = NZ * NPLANE
CW, NC = 512, 4
AG_J, RS_J = 5, 5
TA, TS = 4, 3
LAG = 2
NB = 2


def PARENT(dist, j):
    return 0 if dist == j else dist - 1


def CHILDREN(dist, j):
    return [c for c in range(1, 9) if PARENT(c, j) == dist]


def DEPTH(dist, j):
    return 0 if dist == 0 else 1 + DEPTH(PARENT(dist, j), j)


AG_ORDER = sorted(range(1, 9), key=lambda c: (DEPTH(c, AG_J), c))
RS_ORDER = sorted(range(1, 9), key=lambda c: (-DEPTH(c, RS_J) if c != 8 else -9, -c))
STEPS = sorted({1, AG_J, RS_J})
POS = {0: 0, 8: 15}
for _e, _c in enumerate(AG_ORDER[:-1]):
    POS[NZ - _c], POS[_c] = 1 + 2 * _e, 2 + 2 * _e


def dot(left, right, dims):
    return lax.dot_general(left, right, (dims, ((), ())), preferred_element_type=F32)


def kernel(
    tok_ref, cot_ref, gate_ref, up_ref, down_ref,
    in_out, gate_out, up_out, down_out,
    row, msg, plane, planef, g, wgu, wd, pre, pre_send, pre_recv, act, act_t, hid,
    mine, sib_send, sib_recv, rs_send, rs_recv, fin, fin_recv, line, ogu, od,
    w_sem, p_ss, p_rs, z_ss, z_rs, s_ss, s_rs, y_ss, y_rs, x_ss, x_rs, t_ss, t_rs, r_ss, r_rs, f_ss, f_rs, o_sem,
):
    blk, pair = lax.axis_index("blk"), lax.axis_index("pair")
    z, me, core = blk // NPLANE, lax.rem(blk, NPLANE), lax.rem(blk, 2)
    y = lax.rem(blk // 2, 4)

    def at(zz, pp):
        return (zz * NPLANE + pp, pair)

    def z_at(step):
        return at(lax.rem(z + step + NZ, NZ), me)

    sibling = at(z, me + 1 - 2 * core)
    partner = (blk, 1 - pair)
    spots = [lax.rem(me + k, NPLANE) for k in range(NPLANE)]

    loads = [
        pltpu.make_async_copy(gate_ref, wgu.at[pl.ds(0, UNITS)], w_sem.at[0]),
        pltpu.make_async_copy(up_ref, wgu.at[pl.ds(UNITS, UNITS)], w_sem.at[1]),
        pltpu.make_async_copy(down_ref, wd, w_sem.at[2]),
    ]
    for load in loads:
        load.start()

    barrier = pltpu.get_barrier_semaphore()
    peers = [at(z, spot) for spot in spots[1:]] + [z_at(step) for j in STEPS for step in (j, -j)] + [partner]
    for peer in peers:
        pl.semaphore_signal(barrier, inc=1, device_id=peer, device_id_type=MESH)

    sent = []

    def send(src, dst, ss, rs, to):
        copy = pltpu.make_async_remote_copy(
            src_ref=src, dst_ref=dst, send_sem=ss, recv_sem=rs, device_id=to, device_id_type=MESH
        )
        copy.start()
        sent.append(copy)
        return copy

    for t, ref in enumerate((tok_ref, cot_ref)):
        own = ref[...].astype(F32)
        for s in range(32):
            row[t, s : s + 1, :] = own[:, s * 128 : (s + 1) * 128]
        for h in range(2):
            msg[h, t] = row[t, h * 16 : (h + 1) * 16, :].astype(BF16)
    pl.semaphore_wait(barrier, len(peers))

    swaps = [
        send(msg.at[lax.rem(spots[k], 2)], plane.at[me], p_ss.at[k], p_rs.at[k], at(z, spots[k]))
        for k in range(1, NPLANE)
    ]
    plane[pl.ds(me, 1)] = msg[pl.ds(core, 1)]
    for swap in swaps:
        swap.wait_recv()
    for t in range(2):
        planef[t] = plane[:, t].astype(F32)
        for s in range(16):
            g[core, 0, s, t] = planef[t, :, s, :].astype(BF16)

    hops, crossings, hands = {}, {}, []
    mine_y = TA + TS * y

    def span(d, part, n):
        start, size = (0, TA) if part == 0 else (mine_y, TS)
        if n == 8:
            low = (size + 1) // 2
            return (start, low) if d == 0 else (start + low, size - low)
        return start, size

    def hop(d, src, dst, part):
        start, size = span(d, part, dst)
        e = AG_ORDER.index(dst)
        hops[d, dst, part] = send(
            g.at[core, POS[(-src if d == 0 else src) % NZ], pl.ds(start, size)],
            g.at[core, POS[(-dst if d == 0 else dst) % NZ], pl.ds(start, size)],
            z_ss.at[d, e, part], z_rs.at[d, e, part], z_at(dst - src if d == 0 else src - dst),
        )

    def places(e):
        return pl.ds(1 + 2 * e, 2 if e < 7 else 1)

    def hand(i, where):
        ref = g.at[core, where]
        hands.append(send(ref, ref, s_ss.at[i], s_rs.at[i], sibling))

    def settle(e):
        for m in range(1, 4):
            crossings[e, m].wait_recv()
        hand(e + 1, places(e))

    for part in range(2):
        for first in CHILDREN(0, AG_J):
            for d in range(2):
                hop(d, 0, first, part)
    hand(0, pl.ds(0, 1))
    for e, dist in enumerate(AG_ORDER):
        for part in range(2):
            for d in range(2):
                hops[d, dist, part].wait_recv()
                for child in CHILDREN(dist, AG_J):
                    hop(d, dist, child, part)
        for m in range(1, 4):
            ref = g.at[core, places(e), pl.ds(mine_y, TS)]
            crossings[e, m] = send(ref, ref, y_ss.at[e, m], y_rs.at[e, m], at(z, lax.rem(me + 2 * m, 8) + 8 * (me // 8)))
        if e >= LAG:
            settle(e - LAG)
    for e in range(8 - LAG, 8):
        settle(e)
    for load in loads:
        load.wait()
    for copy in hands:
        copy.wait_recv()

    def rows_of(h, chunk, t):
        return jnp.concatenate([g[h, :, chunk * 4 + j, t].reshape(ROWS, 128) for j in range(4)], axis=1)

    for h in range(2):
        for chunk in range(NC):
            cols = slice(h * HALF + chunk * CW, h * HALF + (chunk + 1) * CW)
            gu = dot(wgu[:, cols], rows_of(h, chunk, 0), ((1,), (1,)))
            dn = dot(wd[:, cols], rows_of(h, chunk, 1), ((1,), (1,)))
            if h == 0 and chunk == 0:
                pre[: 2 * UNITS], pre[2 * UNITS :] = gu, dn
            else:
                pre[: 2 * UNITS] += gu
                pre[2 * UNITS :] += dn
    pre_send[...] = pre[...].astype(BF16)
    send(pre_send, pre_recv, x_ss, x_rs, partner).wait_recv()

    def total(i):
        part = slice(i * UNITS, (i + 1) * UNITS)
        return pre[part] + pre_recv[part].astype(F32)

    gate_act, up_act, hid_grad = total(0), total(1), total(2)
    sigmoid_gate = jax.nn.sigmoid(gate_act)
    silu_gate = gate_act * sigmoid_gate
    hid[...] = (silu_gate * up_act).astype(BF16)
    up_grad = hid_grad * silu_gate
    gate_grad = hid_grad * up_act * sigmoid_gate * (1.0 + gate_act * (1.0 - sigmoid_gate))
    act[:UNITS] = gate_grad.astype(BF16)
    act[UNITS:] = up_grad.astype(BF16)
    act_t[...] = act[...].astype(F32).T.astype(BF16)

    def columns(h, chunk):
        return pl.ds(pl.multiple_of(h * HALF + chunk * CW, CW), CW)

    sides = []
    for chunk in range(NC):
        part = dot(act_t[...], wgu[:, columns(1 - core, chunk)], ((1,), (0,)))
        sib_send[chunk] = part.astype(BF16)
        sides.append(send(sib_send.at[chunk], sib_recv.at[chunk], t_ss.at[chunk], t_rs.at[chunk], sibling))
    for chunk in range(NC):
        mine[chunk] = dot(act_t[...], wgu[:, columns(core, chunk)], ((1,), (0,)))
    for side in sides:
        side.wait_recv()

    def own_part(slot, n):
        here = slice(POS[slot] * 16, POS[slot] * 16 + 16)
        per = NC // NB
        parts = [mine[c, here, :] + sib_recv[c, here, :].astype(F32) for c in range(n * per, (n + 1) * per)]
        return parts[0] if per == 1 else jnp.concatenate(parts, axis=1)

    outs = []

    def weight_chunk(h, chunk):
        i = h * NC + chunk
        cols = slice(i * CW, (i + 1) * CW)
        ogu[:, cols] = dot(act[...], rows_of(h, chunk, 0), ((1,), (0,))).astype(BF16)
        od[:, cols] = dot(hid[...], rows_of(h, chunk, 1), ((1,), (0,))).astype(BF16)
        for j, (src, dst) in enumerate(
            (
                (ogu.at[pl.ds(0, UNITS), cols], gate_out.at[:, cols]),
                (ogu.at[pl.ds(UNITS, UNITS), cols], up_out.at[:, cols]),
                (od.at[:, cols], down_out.at[:, cols]),
            )
        ):
            copy = pltpu.make_async_copy(src, dst, o_sem.at[i, j])
            copy.start()
            outs.append(copy)

    sums = {}

    def collected(d, dist, n):
        value = own_part((dist if d == 0 else -dist) % NZ, n)
        for child in CHILDREN(dist, RS_J):
            if (d, child, n) in sums:
                sums[d, child, n].wait_recv()
                value = value + rs_recv[d, child - 1, n].astype(F32)
        return value

    for e, dist in enumerate(RS_ORDER):
        for n in range(NB):
            for d in range(2):
                if dist == 8 and (n >= NB // 2) != (d == 1):
                    continue
                rs_send[d, dist - 1, n] = collected(d, dist, n).astype(BF16)
                step = dist - PARENT(dist, RS_J)
                sums[d, dist, n] = send(
                    rs_send.at[d, dist - 1, n], rs_recv.at[d, dist - 1, n],
                    r_ss.at[d, dist - 1, n], r_rs.at[d, dist - 1, n], z_at(step if d == 0 else -step),
                )
        weight_chunk(e // NC, e % NC)
    for n in range(NB):
        value = own_part(0, n)
        for d in range(2):
            for child in CHILDREN(0, RS_J):
                sums[d, child, n].wait_recv()
                value = value + rs_recv[d, child - 1, n].astype(F32)
        for s in range(16 // NB):
            fin[:, n * (16 // NB) + s, :] = value[:, s * 128 : (s + 1) * 128]

    last = [
        send(fin.at[spots[k]], fin_recv.at[k], f_ss.at[k], f_rs.at[k], at(z, spots[k])) for k in range(1, NPLANE)
    ]
    halves = [fin[pl.ds(me, 1)].reshape(16, 128), None]
    for k in range(1, NPLANE):
        last[k - 1].wait_recv()
        halves[k % 2] = fin_recv[k] if halves[k % 2] is None else halves[k % 2] + fin_recv[k]
    for i, value in enumerate(halves):
        h = core if i == 0 else 1 - core
        for s in range(16):
            line[0:1, pl.ds(pl.multiple_of(h * HALF + s * 128, 128), 128)] = value[s : s + 1, :]
    in_out[...] = line[...].astype(BF16)
    for copy in sent:
        copy.wait_send()
    for copy in outs:
        copy.wait()


def local(tokens, out_cot, gate_rows, up_rows, down_rows):
    vmem, hbm = pl.BlockSpec(memory_space=pltpu.VMEM), pl.BlockSpec(memory_space=pl.ANY)
    dma = pltpu.SemaphoreType.DMA
    grads = jax.ShapeDtypeStruct((UNITS, WIDTH), BF16)
    return pl.pallas_call(
        kernel,
        out_shape=(jax.ShapeDtypeStruct((1, WIDTH), BF16), grads, grads, grads),
        in_specs=[vmem, vmem, hbm, hbm, hbm],
        out_specs=(vmem, hbm, hbm, hbm),
        scratch_shapes=[
            pltpu.VMEM((2, 32, 128), F32),
            pltpu.VMEM((2, 2, 16, 128), BF16),
            pltpu.VMEM((NPLANE, 2, 16, 128), BF16),
            pltpu.VMEM((2, NPLANE, 16, 128), F32),
            pltpu.VMEM((2, NZ, 16, 2, NPLANE, 128), BF16),
            pltpu.VMEM((2 * UNITS, WIDTH), BF16),
            pltpu.VMEM((UNITS, WIDTH), BF16),
            pltpu.VMEM((3 * UNITS, ROWS), F32),
            pltpu.VMEM((3 * UNITS, ROWS), BF16),
            pltpu.VMEM((3 * UNITS, ROWS), BF16),
            pltpu.VMEM((2 * UNITS, ROWS), BF16),
            pltpu.VMEM((ROWS, 2 * UNITS), BF16),
            pltpu.VMEM((UNITS, ROWS), BF16),
            pltpu.VMEM((NC, ROWS, CW), F32),
            pltpu.VMEM((NC, ROWS, CW), BF16),
            pltpu.VMEM((NC, ROWS, CW), BF16),
            pltpu.VMEM((2, 8, NB, 16, HALF // NB), BF16),
            pltpu.VMEM((2, 8, NB, 16, HALF // NB), BF16),
            pltpu.VMEM((NPLANE, 16, 128), F32),
            pltpu.VMEM((NPLANE, 16, 128), F32),
            pltpu.VMEM((1, WIDTH), F32),
            pltpu.VMEM((2 * UNITS, WIDTH), BF16),
            pltpu.VMEM((UNITS, WIDTH), BF16),
            dma((3,)),
            dma((NPLANE,)), dma((NPLANE,)),
            dma((2, 8, 2)), dma((2, 8, 2)),
            dma((9,)), dma((9,)),
            dma((8, 4)), dma((8, 4)),
            dma, dma,
            dma((NC,)), dma((NC,)),
            dma((2, 8, NB)), dma((2, 8, NB)),
            dma((NPLANE,)), dma((NPLANE,)),
            dma((2 * NC, 3)),
        ],
        compiler_params=pltpu.CompilerParams(
            collective_id=0, has_side_effects=True, vmem_limit_bytes=60 * 1024 * 1024
        ),
        name="swiglu_backward",
    )(tokens, out_cot, gate_rows, up_rows, down_rows)


def solution(mesh):
    specs = (P("blk", "pair"),) * 5
    return jax.shard_map(local, mesh=mesh, in_specs=specs, out_specs=specs[:4], check_vma=False)
```

```python
import functools

import jax
import jax.numpy as jnp
from jax import lax
from jax.experimental import pallas as pl
from jax.experimental.pallas import tpu as pltpu
from jax.sharding import PartitionSpec as P

MESH = pl.DeviceIdType.MESH
F32, BF16 = jnp.float32, jnp.bfloat16
NZ, NPLANE = 16, 16
UNITS, WIDTH, HALF = 96, 4096, 2048
ROWS = NZ * NPLANE
CW, NC = 512, 4
AG_J, RS_J = 5, 5
TA, TS = 4, 3
NB = 2
PARTS = 2


def PARENT(dist, j):
    return 0 if dist == j else dist - 1


def CHILDREN(dist, j):
    return [c for c in range(1, 9) if PARENT(c, j) == dist]


def DEPTH(dist, j):
    return 0 if dist == 0 else 1 + DEPTH(PARENT(dist, j), j)


AG_ORDER = sorted(range(1, 9), key=lambda c: (DEPTH(c, AG_J), c))
RS_ORDER = sorted(range(1, 9), key=lambda c: (-DEPTH(c, RS_J) if c != 8 else -9, -c))
STEPS = sorted({1, AG_J, RS_J})
POS = {0: 0, 8: 15}
for _e, _c in enumerate(AG_ORDER[:-1]):
    POS[NZ - _c], POS[_c] = 1 + 2 * _e, 2 + 2 * _e


def dot(left, right, dims):
    return lax.dot_general(left, right, (dims, ((), ())), preferred_element_type=F32)


def kernel(
    tok_ref, cot_ref, gate_ref, up_ref, down_ref,
    in_out, gate_out, up_out, down_out,
    row, msg, plane, planef, g, w, pre, pre_sib, pre_send, pre_recv, act, act_t,
    mine, rs_send, rs_recv, fin, fin_recv, line, og,
    w_sem, w_ss, w_rs, p_ss, p_rs, z_ss, z_rs, y_ss, y_rs, x_ss, x_rs, t_ss, t_rs, a_ss, a_rs, r_ss, r_rs, f_ss, f_rs, o_ss, o_rs, o_sem,
):
    blk, pair = lax.axis_index("blk"), lax.axis_index("pair")
    z, me, core = blk // NPLANE, lax.rem(blk, NPLANE), lax.rem(blk, 2)
    y = lax.rem(blk // 2, 4)

    def at(zz, pp):
        return (zz * NPLANE + pp, pair)

    def y_at(step):
        return at(z, lax.rem(me + 2 * step, 8) + 8 * (me // 8))

    def z_at(step):
        return at(lax.rem(z + step + NZ, NZ), me)

    sibling = at(z, me + 1 - 2 * core)
    partner = (blk, 1 - pair)
    spots = [lax.rem(me + k, NPLANE) for k in range(NPLANE)]

    def half_of(ref, h):
        return ref.at[:, pl.ds(pl.multiple_of(h * HALF, HALF), HALF)]

    weights = (gate_ref, up_ref, down_ref)
    loads = [pltpu.make_async_copy(half_of(ref, core), w.at[core, i], w_sem.at[i]) for i, ref in enumerate(weights)]
    for load in loads:
        load.start()

    barrier = pltpu.get_barrier_semaphore()
    peers = [at(z, spot) for spot in spots[1:]] + [z_at(step) for j in STEPS for step in (j, -j)] + [partner]
    for peer in peers:
        pl.semaphore_signal(barrier, inc=1, device_id=peer, device_id_type=MESH)

    sent = []

    def send(src, dst, ss, rs, to):
        copy = pltpu.make_async_remote_copy(
            src_ref=src, dst_ref=dst, send_sem=ss, recv_sem=rs, device_id=to, device_id_type=MESH
        )
        copy.start()
        sent.append(copy)
        return copy

    for t, ref in enumerate((tok_ref, cot_ref)):
        own = ref[...].astype(F32)
        for s in range(32):
            row[t, s : s + 1, :] = own[:, s * 128 : (s + 1) * 128]
        for h in range(2):
            msg[h, t] = row[t, h * 16 : (h + 1) * 16, :].astype(BF16)
    pl.semaphore_wait(barrier, len(peers))

    swaps = [
        send(msg.at[lax.rem(spots[k], 2)], plane.at[me], p_ss.at[k], p_rs.at[k], at(z, spots[k]))
        for k in range(1, NPLANE)
    ]
    lent = [
        send(half_of(ref, 1 - core), w.at[core, i], w_ss.at[i], w_rs.at[i], sibling) for i, ref in enumerate(weights)
    ]
    plane[pl.ds(me, 1)] = msg[pl.ds(core, 1)]
    for swap in swaps:
        swap.wait_recv()
    for t in range(2):
        planef[t] = plane[:, t].astype(F32)
        for s in range(16):
            g[0, s, t] = planef[t, :, s, :].astype(BF16)

    hops, crossings = {}, {}
    mine_y = TA + TS * y

    def span(d, part, n):
        start, size = (0, TA) if part == 0 else (mine_y, TS)
        if n == 8:
            low = (size + 1) // 2
            return (start, low) if d == 0 else (start + low, size - low)
        return start, size

    def hop(d, src, dst, part):
        start, size = span(d, part, dst)
        e = AG_ORDER.index(dst)
        hops[d, dst, part] = send(
            g.at[POS[(-src if d == 0 else src) % NZ], pl.ds(start, size)],
            g.at[POS[(-dst if d == 0 else dst) % NZ], pl.ds(start, size)],
            z_ss.at[d, e, part], z_rs.at[d, e, part], z_at(dst - src if d == 0 else src - dst),
        )

    def places(e):
        return pl.ds(1 + 2 * e, 2 if e < 7 else 1)

    for part in (1, 0):
        for first in CHILDREN(0, AG_J):
            for d in range(2):
                hop(d, 0, first, part)
    for e, dist in enumerate(AG_ORDER):
        for part in (1, 0):
            for d in range(2):
                hops[d, dist, part].wait_recv()
                for child in CHILDREN(dist, AG_J):
                    hop(d, dist, child, part)
            if part == 1:
                for m in range(1, 4):
                    ref = g.at[places(e), pl.ds(mine_y, TS)]
                    crossings[e, m] = send(ref, ref, y_ss.at[e, m], y_rs.at[e, m], y_at(m))
    for load in loads:
        load.wait()
    for loan in lent:
        loan.wait_recv()

    def rows_of(chunk, t, start=0, size=NZ):
        return jnp.concatenate(
            [g[start : start + size, chunk * 4 + j, t].reshape(size * NPLANE, 128) for j in range(4)], axis=1
        )

    def partial(i, u):
        for chunk in range(NC):
            cols = slice(chunk * CW, (chunk + 1) * CW)
            gu = dot(w[u, :2, :, cols].reshape(2 * UNITS, CW), rows_of(chunk, 0, 8 * i, 8), ((1,), (1,)))
            dn = dot(w[u, 2, :, cols], rows_of(chunk, 1, 8 * i, 8), ((1,), (1,)))
            if chunk == 0:
                pre[i, u, : 2 * UNITS], pre[i, u, 2 * UNITS :] = gu, dn
            else:
                pre[i, u, : 2 * UNITS] += gu
                pre[i, u, 2 * UNITS :] += dn

    def begin(i):
        partial(i, 1 - core)
        swap = send(pre.at[i, 1 - core], pre_sib.at[i], t_ss.at[i], t_rs.at[i], sibling)
        partial(i, core)
        return swap

    def pair_up(i, swap):
        swap.wait_recv()
        pre_sib[i] = pre_sib[i] + pre[i, core]
        pre_send[i] = pre_sib[i].astype(BF16)
        return send(pre_send.at[i], pre_recv.at[i], x_ss.at[i], x_rs.at[i], partner)

    def finish(i, copy):
        copy.wait_recv()
        parts = [slice(j * UNITS, (j + 1) * UNITS) for j in range(3)]
        gate_act, up_act, hid_grad = [pre_sib[i, part] + pre_recv[i, part].astype(F32) for part in parts]
        sigmoid_gate = jax.nn.sigmoid(gate_act)
        silu_gate = gate_act * sigmoid_gate
        here = slice(i * ROWS // 2, (i + 1) * ROWS // 2)
        gate_grad = hid_grad * up_act * sigmoid_gate * (1.0 + gate_act * (1.0 - sigmoid_gate))
        act[core, parts[0], here] = gate_grad.astype(BF16)
        act[core, parts[1], here] = (hid_grad * silu_gate).astype(BF16)
        act[core, parts[2], here] = (silu_gate * up_act).astype(BF16)

    for (e, _), crossing in crossings.items():
        if e < 4:
            crossing.wait_recv()
    early = pair_up(0, begin(0))
    for (e, _), crossing in crossings.items():
        if e >= 4:
            crossing.wait_recv()
    swap = begin(1)
    finish(0, early)
    finish(1, pair_up(1, swap))
    swap = send(act.at[core], act.at[core], a_ss, a_rs, sibling)

    def input_part(u):
        act_t[...] = act[u, : 2 * UNITS].astype(F32).T.astype(BF16)
        for chunk in range(NC):
            cols = slice(chunk * CW, (chunk + 1) * CW)
            yield chunk, dot(act_t[...], w[u, :2, :, cols].reshape(2 * UNITS, CW), ((1,), (0,)))

    for chunk, part in input_part(core):
        mine[chunk] = part
    swap.wait_recv()
    for chunk, part in input_part(1 - core):
        mine[chunk] += part

    def own_part(slot, n):
        here = slice(POS[slot] * 16, POS[slot] * 16 + 16)
        per = NC // NB
        parts = [mine[c, here, :] for c in range(n * per, (n + 1) * per)]
        return parts[0] if per == 1 else jnp.concatenate(parts, axis=1)

    outs = []

    def weight_chunk(k, chunk):
        u = 1 - core if k == 0 else core
        cols = slice(chunk * CW, (chunk + 1) * CW)
        there = pl.ds(pl.multiple_of(core * HALF + chunk * CW, CW), CW)
        gu = dot(act[u, : 2 * UNITS], rows_of(chunk, 0), ((1,), (0,))).astype(BF16)
        og[k, 0, :, cols], og[k, 1, :, cols] = gu[:UNITS], gu[UNITS:]
        og[k, 2, :, cols] = dot(act[u, 2 * UNITS :], rows_of(chunk, 1), ((1,), (0,))).astype(BF16)
        for j, ref in enumerate((gate_out, up_out, down_out)):
            src, dst = og.at[k, j, :, cols], ref.at[:, there]
            if k == 0:
                outs.append(send(src, dst, o_ss.at[chunk, j], o_rs.at[chunk, j], sibling))
            else:
                copy = pltpu.make_async_copy(src, dst, o_sem.at[chunk, j])
                copy.start()
                outs.append(copy)

    sums = {}

    def collected(d, dist, n):
        value = own_part((dist if d == 0 else -dist) % NZ, n)
        for child in CHILDREN(dist, RS_J):
            if (d, child, n) in sums:
                sums[d, child, n].wait_recv()
                value = value + rs_recv[d, child - 1, n].astype(F32)
        return value

    for e, dist in enumerate(RS_ORDER):
        for n in range(NB):
            for d in range(2):
                if dist == 8 and (n >= NB // 2) != (d == 1):
                    continue
                rs_send[d, dist - 1, n] = collected(d, dist, n).astype(BF16)
                step = dist - PARENT(dist, RS_J)
                sums[d, dist, n] = send(
                    rs_send.at[d, dist - 1, n], rs_recv.at[d, dist - 1, n],
                    r_ss.at[d, dist - 1, n], r_rs.at[d, dist - 1, n], z_at(step if d == 0 else -step),
                )
        weight_chunk(e // NC, e % NC)
    for n in range(NB):
        value = own_part(0, n)
        for d in range(2):
            for child in CHILDREN(0, RS_J):
                sums[d, child, n].wait_recv()
                value = value + rs_recv[d, child - 1, n].astype(F32)
        for s in range(16 // NB):
            fin[:, n * (16 // NB) + s, :] = value[:, s * 128 : (s + 1) * 128]

    last = [
        send(fin.at[spots[k]], fin_recv.at[k], f_ss.at[k], f_rs.at[k], at(z, spots[k])) for k in range(1, NPLANE)
    ]
    halves = [fin[pl.ds(me, 1)].reshape(16, 128), None]
    for k in range(1, NPLANE):
        last[k - 1].wait_recv()
        halves[k % 2] = fin_recv[k] if halves[k % 2] is None else halves[k % 2] + fin_recv[k]
    for i, value in enumerate(halves):
        h = core if i == 0 else 1 - core
        for s in range(16):
            line[0:1, pl.ds(pl.multiple_of(h * HALF + s * 128, 128), 128)] = value[s : s + 1, :]
    in_out[...] = line[...].astype(BF16)
    for copy in sent:
        copy.wait_send()
    for i, copy in enumerate(outs):
        if i < len(outs) // 2:
            copy.wait_recv()
        else:
            copy.wait()


def publish(*refs):
    for src, dst in zip(refs[:4], refs[4:]):
        dst[...] = src[...]


def local(tokens, out_cot, gate_rows, up_rows, down_rows):
    vmem, hbm = pl.BlockSpec(memory_space=pltpu.VMEM), pl.BlockSpec(memory_space=pl.ANY)
    dma = pltpu.SemaphoreType.DMA
    grads = jax.ShapeDtypeStruct((UNITS, WIDTH), BF16)
    shapes = (jax.ShapeDtypeStruct((1, WIDTH), BF16), grads, grads, grads)
    results = pl.pallas_call(
        kernel,
        out_shape=shapes,
        in_specs=[vmem, vmem, hbm, hbm, hbm],
        out_specs=(vmem, hbm, hbm, hbm),
        scratch_shapes=[
            pltpu.VMEM((2, 32, 128), F32),
            pltpu.VMEM((2, 2, 16, 128), BF16),
            pltpu.VMEM((NPLANE, 2, 16, 128), BF16),
            pltpu.VMEM((2, NPLANE, 16, 128), F32),
            pltpu.VMEM((NZ, 16, 2, NPLANE, 128), BF16),
            pltpu.VMEM((2, 3, UNITS, HALF), BF16),
            pltpu.VMEM((2, 2, 3 * UNITS, ROWS // 2), F32),
            pltpu.VMEM((2, 3 * UNITS, ROWS // 2), F32),
            pltpu.VMEM((2, 3 * UNITS, ROWS // 2), BF16),
            pltpu.VMEM((2, 3 * UNITS, ROWS // 2), BF16),
            pltpu.VMEM((2, 3 * UNITS, ROWS), BF16),
            pltpu.VMEM((ROWS, 2 * UNITS), BF16),
            pltpu.VMEM((NC, ROWS, CW), F32),
            pltpu.VMEM((2, 8, NB, 16, HALF // NB), BF16),
            pltpu.VMEM((2, 8, NB, 16, HALF // NB), BF16),
            pltpu.VMEM((NPLANE, 16, 128), F32),
            pltpu.VMEM((NPLANE, 16, 128), F32),
            pltpu.VMEM((1, WIDTH), F32),
            pltpu.VMEM((2, 3, UNITS, HALF), BF16),
            dma((3,)), dma((3,)), dma((3,)),
            dma((NPLANE,)), dma((NPLANE,)),
            dma((2, 8, 2)), dma((2, 8, 2)),
            dma((8, 4)), dma((8, 4)),
            dma((2,)), dma((2,)),
            dma((2,)), dma((2,)),
            dma, dma,
            dma((2, 8, NB)), dma((2, 8, NB)),
            dma((NPLANE,)), dma((NPLANE,)),
            dma((NC, 3)), dma((NC, 3)), dma((NC, 3)),
        ],
        compiler_params=pltpu.CompilerParams(
            collective_id=0, has_side_effects=True, vmem_limit_bytes=60 * 1024 * 1024
        ),
        name="swiglu_backward",
    )(tokens, out_cot, gate_rows, up_rows, down_rows)
    line = pl.BlockSpec((1, WIDTH), lambda i: (0, 0))
    rows = pl.BlockSpec((UNITS // PARTS, WIDTH), lambda i: (i, 0))
    return pl.pallas_call(
        publish,
        out_shape=shapes,
        grid=(PARTS,),
        in_specs=[line, rows, rows, rows],
        out_specs=(line, rows, rows, rows),
        compiler_params=pltpu.CompilerParams(vmem_limit_bytes=60 * 1024 * 1024),
        name="publish",
    )(*results)


def solution(mesh):
    specs = (P("blk", "pair"),) * 5
    return jax.shard_map(local, mesh=mesh, in_specs=specs, out_specs=specs[:4], check_vma=False)
```

```python
import functools

import jax
import jax.numpy as jnp
from jax import lax
from jax.experimental import pallas as pl
from jax.experimental.pallas import tpu as pltpu
from jax.sharding import PartitionSpec as P

MESH = pl.DeviceIdType.MESH
F32, BF16 = jnp.float32, jnp.bfloat16
NZ, NPLANE = 16, 16
UNITS, WIDTH, HALF = 96, 4096, 2048
ROWS = NZ * NPLANE
CW, NC = 512, 4
AG_J, RS_J = 5, 5
TA, TS = 4, 3
NB = 2
PARTS = 2


def PARENT(dist, j):
    return 0 if dist == j else dist - 1


def CHILDREN(dist, j):
    return [c for c in range(1, 9) if PARENT(c, j) == dist]


def DEPTH(dist, j):
    return 0 if dist == 0 else 1 + DEPTH(PARENT(dist, j), j)


AG_ORDER = sorted(range(1, 9), key=lambda c: (DEPTH(c, AG_J), c))
RS_ORDER = sorted(range(1, 9), key=lambda c: (-DEPTH(c, RS_J) if c != 8 else -9, -c))
STEPS = sorted({1, AG_J, RS_J})
POS = {0: 0, 8: 15}
for _e, _c in enumerate(AG_ORDER[:-1]):
    POS[NZ - _c], POS[_c] = 1 + 2 * _e, 2 + 2 * _e


def dot(left, right, dims):
    return lax.dot_general(left, right, (dims, ((), ())), preferred_element_type=F32)


def kernel(
    tok_ref, cot_ref, gate_ref, up_ref, down_ref,
    in_out, gate_out, up_out, down_out,
    row, msg, plane, planef, g, w, pre, pre_sib, pre_send, pre_recv, act, act_t,
    mine, rs_send, rs_recv, fin, fin_recv, line, og,
    w_sem, w_ss, w_rs, p_ss, p_rs, z_ss, z_rs, y_ss, y_rs, x_ss, x_rs, t_ss, t_rs, a_ss, a_rs, r_ss, r_rs, f_ss, f_rs, o_ss, o_rs, o_sem,
):
    blk, pair = lax.axis_index("blk"), lax.axis_index("pair")
    z, me, core = blk // NPLANE, lax.rem(blk, NPLANE), lax.rem(blk, 2)
    y = lax.rem(blk // 2, 4)

    def at(zz, pp):
        return (zz * NPLANE + pp, pair)

    def y_at(step):
        return at(z, lax.rem(me + 2 * step, 8) + 8 * (me // 8))

    def z_at(step):
        return at(lax.rem(z + step + NZ, NZ), me)

    sibling = at(z, me + 1 - 2 * core)
    partner = (blk, 1 - pair)
    spots = [lax.rem(me + k, NPLANE) for k in range(NPLANE)]

    def half_of(ref, h):
        return ref.at[:, pl.ds(pl.multiple_of(h * HALF, HALF), HALF)]

    weights = (gate_ref, up_ref, down_ref)
    loads = [pltpu.make_async_copy(half_of(ref, core), w.at[core, i], w_sem.at[i]) for i, ref in enumerate(weights)]
    for load in loads:
        load.start()

    barrier = pltpu.get_barrier_semaphore()
    peers = [at(z, spot) for spot in spots[1:]] + [z_at(step) for j in STEPS for step in (j, -j)] + [partner]
    for peer in peers:
        pl.semaphore_signal(barrier, inc=1, device_id=peer, device_id_type=MESH)

    sent, done = [], []

    def drain(count):
        while len(done) < count:
            sent[len(done)].wait_send()
            done.append(True)

    def send(src, dst, ss, rs, to):
        copy = pltpu.make_async_remote_copy(
            src_ref=src, dst_ref=dst, send_sem=ss, recv_sem=rs, device_id=to, device_id_type=MESH
        )
        copy.start()
        sent.append(copy)
        return copy

    for t, ref in enumerate((tok_ref, cot_ref)):
        own = ref[...].astype(F32)
        for s in range(32):
            row[t, s : s + 1, :] = own[:, s * 128 : (s + 1) * 128]
        for h in range(2):
            msg[h, t] = row[t, h * 16 : (h + 1) * 16, :].astype(BF16)
    pl.semaphore_wait(barrier, len(peers))

    swaps = [
        send(msg.at[lax.rem(spots[k], 2)], plane.at[me], p_ss.at[k], p_rs.at[k], at(z, spots[k]))
        for k in range(1, NPLANE)
    ]
    lent = [
        send(half_of(ref, 1 - core), w.at[core, i], w_ss.at[i], w_rs.at[i], sibling) for i, ref in enumerate(weights)
    ]
    plane[pl.ds(me, 1)] = msg[pl.ds(core, 1)]
    for swap in swaps:
        swap.wait_recv()
    for t in range(2):
        planef[t] = plane[:, t].astype(F32)
        for s in range(16):
            g[0, s, t] = planef[t, :, s, :].astype(BF16)

    hops, crossings = {}, {}
    mine_y = TA + TS * y

    def span(d, part, n):
        start, size = (0, TA) if part == 0 else (mine_y, TS)
        if n == 8:
            low = (size + 1) // 2
            return (start, low) if d == 0 else (start + low, size - low)
        return start, size

    def hop(d, src, dst, part):
        start, size = span(d, part, dst)
        e = AG_ORDER.index(dst)
        hops[d, dst, part] = send(
            g.at[POS[(-src if d == 0 else src) % NZ], pl.ds(start, size)],
            g.at[POS[(-dst if d == 0 else dst) % NZ], pl.ds(start, size)],
            z_ss.at[d, e, part], z_rs.at[d, e, part], z_at(dst - src if d == 0 else src - dst),
        )

    def places(e):
        return pl.ds(1 + 2 * e, 2 if e < 7 else 1)

    for part in (1, 0):
        for first in CHILDREN(0, AG_J):
            for d in range(2):
                hop(d, 0, first, part)
    for e, dist in enumerate(AG_ORDER):
        for part in (1, 0):
            for d in range(2):
                hops[d, dist, part].wait_recv()
                for child in CHILDREN(dist, AG_J):
                    hop(d, dist, child, part)
            if part == 1:
                for m in range(1, 4):
                    ref = g.at[places(e), pl.ds(mine_y, TS)]
                    crossings[e, m] = send(ref, ref, y_ss.at[e, m], y_rs.at[e, m], y_at(m))
    for load in loads:
        load.wait()
    for loan in lent:
        loan.wait_recv()

    def rows_of(chunk, t, start=0, size=NZ):
        return jnp.concatenate(
            [g[start : start + size, chunk * 4 + j, t].reshape(size * NPLANE, 128) for j in range(4)], axis=1
        )

    def partial(i, u):
        for chunk in range(NC):
            cols = slice(chunk * CW, (chunk + 1) * CW)
            gu = dot(w[u, :2, :, cols].reshape(2 * UNITS, CW), rows_of(chunk, 0, 8 * i, 8), ((1,), (1,)))
            dn = dot(w[u, 2, :, cols], rows_of(chunk, 1, 8 * i, 8), ((1,), (1,)))
            if chunk == 0:
                pre[i, u, : 2 * UNITS], pre[i, u, 2 * UNITS :] = gu, dn
            else:
                pre[i, u, : 2 * UNITS] += gu
                pre[i, u, 2 * UNITS :] += dn

    def begin(i):
        partial(i, 1 - core)
        swap = send(pre.at[i, 1 - core], pre_sib.at[i], t_ss.at[i], t_rs.at[i], sibling)
        partial(i, core)
        return swap

    def pair_up(i, swap):
        swap.wait_recv()
        pre_sib[i] = pre_sib[i] + pre[i, core]
        pre_send[i] = pre_sib[i].astype(BF16)
        return send(pre_send.at[i], pre_recv.at[i], x_ss.at[i], x_rs.at[i], partner)

    def finish(i, copy):
        copy.wait_recv()
        parts = [slice(j * UNITS, (j + 1) * UNITS) for j in range(3)]
        gate_act, up_act, hid_grad = [pre_sib[i, part] + pre_recv[i, part].astype(F32) for part in parts]
        sigmoid_gate = jax.nn.sigmoid(gate_act)
        silu_gate = gate_act * sigmoid_gate
        here = slice(i * ROWS // 2, (i + 1) * ROWS // 2)
        gate_grad = hid_grad * up_act * sigmoid_gate * (1.0 + gate_act * (1.0 - sigmoid_gate))
        act[core, parts[0], here] = gate_grad.astype(BF16)
        act[core, parts[1], here] = (hid_grad * silu_gate).astype(BF16)
        act[core, parts[2], here] = (silu_gate * up_act).astype(BF16)

    for (e, _), crossing in crossings.items():
        if e < 4:
            crossing.wait_recv()
    early = pair_up(0, begin(0))
    for (e, _), crossing in crossings.items():
        if e >= 4:
            crossing.wait_recv()
    swap = begin(1)
    finish(0, early)
    finish(1, pair_up(1, swap))
    swap = send(act.at[core], act.at[core], a_ss, a_rs, sibling)

    def input_part(u):
        act_t[...] = act[u, : 2 * UNITS].astype(F32).T.astype(BF16)
        for chunk in range(NC):
            cols = slice(chunk * CW, (chunk + 1) * CW)
            yield chunk, dot(act_t[...], w[u, :2, :, cols].reshape(2 * UNITS, CW), ((1,), (0,)))

    for chunk, part in input_part(core):
        mine[chunk] = part
    swap.wait_recv()
    for chunk, part in input_part(1 - core):
        mine[chunk] += part

    def own_part(slot, n):
        here = slice(POS[slot] * 16, POS[slot] * 16 + 16)
        per = NC // NB
        parts = [mine[c, here, :] for c in range(n * per, (n + 1) * per)]
        return parts[0] if per == 1 else jnp.concatenate(parts, axis=1)

    outs = []

    def weight_chunk(k, chunk):
        u = 1 - core if k == 0 else core
        cols = slice(chunk * CW, (chunk + 1) * CW)
        there = pl.ds(pl.multiple_of(core * HALF + chunk * CW, CW), CW)
        gu = dot(act[u, : 2 * UNITS], rows_of(chunk, 0), ((1,), (0,))).astype(BF16)
        og[k, 0, :, cols], og[k, 1, :, cols] = gu[:UNITS], gu[UNITS:]
        og[k, 2, :, cols] = dot(act[u, 2 * UNITS :], rows_of(chunk, 1), ((1,), (0,))).astype(BF16)
        for j, ref in enumerate((gate_out, up_out, down_out)):
            src, dst = og.at[k, j, :, cols], ref.at[:, there]
            if k == 0:
                outs.append(send(src, dst, o_ss.at[chunk, j], o_rs.at[chunk, j], sibling))
            else:
                copy = pltpu.make_async_copy(src, dst, o_sem.at[chunk, j])
                copy.start()
                outs.append(copy)

    sums = {}

    def collected(d, dist, n):
        value = own_part((dist if d == 0 else -dist) % NZ, n)
        for child in CHILDREN(dist, RS_J):
            if (d, child, n) in sums:
                sums[d, child, n].wait_recv()
                value = value + rs_recv[d, child - 1, n].astype(F32)
        return value

    before = len(sent)
    for e, dist in enumerate(RS_ORDER):
        for n in range(NB):
            for d in range(2):
                if dist == 8 and (n >= NB // 2) != (d == 1):
                    continue
                rs_send[d, dist - 1, n] = collected(d, dist, n).astype(BF16)
                step = dist - PARENT(dist, RS_J)
                sums[d, dist, n] = send(
                    rs_send.at[d, dist - 1, n], rs_recv.at[d, dist - 1, n],
                    r_ss.at[d, dist - 1, n], r_rs.at[d, dist - 1, n], z_at(step if d == 0 else -step),
                )
        weight_chunk(e // NC, e % NC)
        drain(before * (e + 1) // 8)
    for n in range(NB):
        value = own_part(0, n)
        for d in range(2):
            for child in CHILDREN(0, RS_J):
                sums[d, child, n].wait_recv()
                value = value + rs_recv[d, child - 1, n].astype(F32)
        for s in range(16 // NB):
            fin[:, n * (16 // NB) + s, :] = value[:, s * 128 : (s + 1) * 128]

    last = [
        send(fin.at[spots[k]], fin_recv.at[k], f_ss.at[k], f_rs.at[k], at(z, spots[k])) for k in range(1, NPLANE)
    ]
    drain(len(sent) - len(last))
    for i, copy in enumerate(outs):
        if i < len(outs) // 2:
            copy.wait_recv()
        else:
            copy.wait()
    halves = [fin[pl.ds(me, 1)].reshape(16, 128), None]
    for k in range(1, NPLANE):
        last[k - 1].wait_recv()
        halves[k % 2] = fin_recv[k] if halves[k % 2] is None else halves[k % 2] + fin_recv[k]
    for i, value in enumerate(halves):
        h = core if i == 0 else 1 - core
        for s in range(16):
            line[0:1, pl.ds(pl.multiple_of(h * HALF + s * 128, 128), 128)] = value[s : s + 1, :]
    in_out[...] = line[...].astype(BF16)
    drain(len(sent))


def publish(*refs):
    for src, dst in zip(refs[:4], refs[4:]):
        dst[...] = src[...]


def local(tokens, out_cot, gate_rows, up_rows, down_rows):
    vmem, hbm = pl.BlockSpec(memory_space=pltpu.VMEM), pl.BlockSpec(memory_space=pl.ANY)
    dma = pltpu.SemaphoreType.DMA
    grads = jax.ShapeDtypeStruct((UNITS, WIDTH), BF16)
    shapes = (jax.ShapeDtypeStruct((1, WIDTH), BF16), grads, grads, grads)
    results = pl.pallas_call(
        kernel,
        out_shape=shapes,
        in_specs=[vmem, vmem, hbm, hbm, hbm],
        out_specs=(vmem, hbm, hbm, hbm),
        scratch_shapes=[
            pltpu.VMEM((2, 32, 128), F32),
            pltpu.VMEM((2, 2, 16, 128), BF16),
            pltpu.VMEM((NPLANE, 2, 16, 128), BF16),
            pltpu.VMEM((2, NPLANE, 16, 128), F32),
            pltpu.VMEM((NZ, 16, 2, NPLANE, 128), BF16),
            pltpu.VMEM((2, 3, UNITS, HALF), BF16),
            pltpu.VMEM((2, 2, 3 * UNITS, ROWS // 2), F32),
            pltpu.VMEM((2, 3 * UNITS, ROWS // 2), F32),
            pltpu.VMEM((2, 3 * UNITS, ROWS // 2), BF16),
            pltpu.VMEM((2, 3 * UNITS, ROWS // 2), BF16),
            pltpu.VMEM((2, 3 * UNITS, ROWS), BF16),
            pltpu.VMEM((ROWS, 2 * UNITS), BF16),
            pltpu.VMEM((NC, ROWS, CW), F32),
            pltpu.VMEM((2, 8, NB, 16, HALF // NB), BF16),
            pltpu.VMEM((2, 8, NB, 16, HALF // NB), BF16),
            pltpu.VMEM((NPLANE, 16, 128), F32),
            pltpu.VMEM((NPLANE, 16, 128), F32),
            pltpu.VMEM((1, WIDTH), F32),
            pltpu.VMEM((2, 3, UNITS, HALF), BF16),
            dma((3,)), dma((3,)), dma((3,)),
            dma((NPLANE,)), dma((NPLANE,)),
            dma((2, 8, 2)), dma((2, 8, 2)),
            dma((8, 4)), dma((8, 4)),
            dma((2,)), dma((2,)),
            dma((2,)), dma((2,)),
            dma, dma,
            dma((2, 8, NB)), dma((2, 8, NB)),
            dma((NPLANE,)), dma((NPLANE,)),
            dma((NC, 3)), dma((NC, 3)), dma((NC, 3)),
        ],
        compiler_params=pltpu.CompilerParams(
            collective_id=0, has_side_effects=True, vmem_limit_bytes=60 * 1024 * 1024
        ),
        name="swiglu_backward",
    )(tokens, out_cot, gate_rows, up_rows, down_rows)
    line = pl.BlockSpec((1, WIDTH), lambda i: (0, 0))
    rows = pl.BlockSpec((UNITS // PARTS, WIDTH), lambda i: (i, 0))
    return pl.pallas_call(
        publish,
        out_shape=shapes,
        grid=(PARTS,),
        in_specs=[line, rows, rows, rows],
        out_specs=(line, rows, rows, rows),
        compiler_params=pltpu.CompilerParams(vmem_limit_bytes=60 * 1024 * 1024),
        name="publish",
    )(*results)


def solution(mesh):
    specs = (P("blk", "pair"),) * 5
    return jax.shard_map(local, mesh=mesh, in_specs=specs, out_specs=specs[:4], check_vma=False)
```

```python
import functools

import jax
import jax.numpy as jnp
from jax import lax
from jax.experimental import pallas as pl
from jax.experimental.pallas import tpu as pltpu
from jax.sharding import PartitionSpec as P

MESH = pl.DeviceIdType.MESH
F32, BF16 = jnp.float32, jnp.bfloat16
NZ, NPLANE = 16, 16
UNITS, WIDTH, HALF = 96, 4096, 2048
ROWS = NZ * NPLANE
CW, NC = 512, 4
AG_J, RS_J = 5, 5
TA, TS = 4, 3
NB = 2
PARTS = 2


def PARENT(dist, j):
    return 0 if dist == j else dist - 1


def CHILDREN(dist, j):
    return [c for c in range(1, 9) if PARENT(c, j) == dist]


def DEPTH(dist, j):
    return 0 if dist == 0 else 1 + DEPTH(PARENT(dist, j), j)


AG_ORDER = sorted(range(1, 9), key=lambda c: (DEPTH(c, AG_J), c))
RS_ORDER = sorted(range(1, 9), key=lambda c: (-DEPTH(c, RS_J) if c != 8 else -9, -c))
STEPS = sorted({1, AG_J, RS_J})
POS = {0: 0, 8: 15}
for _e, _c in enumerate(AG_ORDER[:-1]):
    POS[NZ - _c], POS[_c] = 1 + 2 * _e, 2 + 2 * _e


def dot(left, right, dims):
    return lax.dot_general(left, right, (dims, ((), ())), preferred_element_type=F32)


def kernel(
    tok_ref, cot_ref, gate_ref, up_ref, down_ref,
    in_out, gate_out, up_out, down_out,
    tok_row, cot_row, row, msg, plane, planef, g, w, pre, pre_sib, pre_send, pre_recv, act, act_t,
    mine, rs_send, rs_recv, fin, fin_recv, line, og,
    own_sem, w_sem, w_ss, w_rs, p_ss, p_rs, z_ss, z_rs, y_ss, y_rs, x_ss, x_rs, t_ss, t_rs, a_ss, a_rs, r_ss, r_rs, f_ss, f_rs, o_ss, o_rs, o_sem,
):
    blk, pair = lax.axis_index("blk"), lax.axis_index("pair")
    z, me, core = blk // NPLANE, lax.rem(blk, NPLANE), lax.rem(blk, 2)
    y = lax.rem(blk // 2, 4)

    def at(zz, pp):
        return (zz * NPLANE + pp, pair)

    def y_at(step):
        return at(z, lax.rem(me + 2 * step, 8) + 8 * (me // 8))

    def z_at(step):
        return at(lax.rem(z + step + NZ, NZ), me)

    sibling = at(z, me + 1 - 2 * core)
    partner = (blk, 1 - pair)
    spots = [lax.rem(me + k, NPLANE) for k in range(NPLANE)]

    def half_of(ref, h):
        return ref.at[:, pl.ds(pl.multiple_of(h * HALF, HALF), HALF)]

    weights = (gate_ref, up_ref, down_ref)
    loads = [pltpu.make_async_copy(half_of(ref, core), w.at[core, i], w_sem.at[i]) for i, ref in enumerate(weights)]
    barrier = pltpu.get_barrier_semaphore()
    peers = [at(z, spot) for spot in spots[1:]] + [z_at(step) for j in STEPS for step in (j, -j)] + [partner]
    for peer in peers:
        pl.semaphore_signal(barrier, inc=1, device_id=peer, device_id_type=MESH)
    owns = [
        pltpu.make_async_copy(tok_ref, tok_row, own_sem.at[0]), pltpu.make_async_copy(cot_ref, cot_row, own_sem.at[1])
    ]
    for load in owns + loads:
        load.start()

    sent, done = [], []

    def drain(count):
        while len(done) < count:
            sent[len(done)].wait_send()
            done.append(True)

    def send(src, dst, ss, rs, to):
        copy = pltpu.make_async_remote_copy(
            src_ref=src, dst_ref=dst, send_sem=ss, recv_sem=rs, device_id=to, device_id_type=MESH
        )
        copy.start()
        sent.append(copy)
        return copy

    for own in owns:
        own.wait()
    for t, ref in enumerate((tok_row, cot_row)):
        own = ref[...].astype(F32)
        for s in range(32):
            row[t, s : s + 1, :] = own[:, s * 128 : (s + 1) * 128]
        for h in range(2):
            msg[h, t] = row[t, h * 16 : (h + 1) * 16, :].astype(BF16)
    pl.semaphore_wait(barrier, len(peers))

    swaps = [
        send(msg.at[lax.rem(spots[k], 2)], plane.at[me], p_ss.at[k], p_rs.at[k], at(z, spots[k]))
        for k in range(1, NPLANE)
    ]
    lent = [
        send(half_of(ref, 1 - core), w.at[core, i], w_ss.at[i], w_rs.at[i], sibling) for i, ref in enumerate(weights)
    ]
    plane[pl.ds(me, 1)] = msg[pl.ds(core, 1)]
    for swap in swaps:
        swap.wait_recv()
    for t in range(2):
        planef[t] = plane[:, t].astype(F32)
        for s in range(16):
            g[0, s, t] = planef[t, :, s, :].astype(BF16)

    hops, crossings = {}, {}
    mine_y = TA + TS * y

    def span(d, part, n):
        start, size = (0, TA) if part == 0 else (mine_y, TS)
        if n == 8:
            low = (size + 1) // 2
            return (start, low) if d == 0 else (start + low, size - low)
        return start, size

    def hop(d, src, dst, part):
        start, size = span(d, part, dst)
        e = AG_ORDER.index(dst)
        hops[d, dst, part] = send(
            g.at[POS[(-src if d == 0 else src) % NZ], pl.ds(start, size)],
            g.at[POS[(-dst if d == 0 else dst) % NZ], pl.ds(start, size)],
            z_ss.at[d, e, part], z_rs.at[d, e, part], z_at(dst - src if d == 0 else src - dst),
        )

    def places(e):
        return pl.ds(1 + 2 * e, 2 if e < 7 else 1)

    for part in (1, 0):
        for first in CHILDREN(0, AG_J):
            for d in range(2):
                hop(d, 0, first, part)
    for e, dist in enumerate(AG_ORDER):
        for part in (1, 0):
            for d in range(2):
                hops[d, dist, part].wait_recv()
                for child in CHILDREN(dist, AG_J):
                    hop(d, dist, child, part)
            if part == 1:
                for m in range(1, 4):
                    ref = g.at[places(e), pl.ds(mine_y, TS)]
                    crossings[e, m] = send(ref, ref, y_ss.at[e, m], y_rs.at[e, m], y_at(m))
    for load in loads:
        load.wait()
    for loan in lent:
        loan.wait_recv()

    def rows_of(chunk, t, start=0, size=NZ):
        return jnp.concatenate(
            [g[start : start + size, chunk * 4 + j, t].reshape(size * NPLANE, 128) for j in range(4)], axis=1
        )

    def partial(i, u):
        for chunk in range(NC):
            cols = slice(chunk * CW, (chunk + 1) * CW)
            gu = dot(w[u, :2, :, cols].reshape(2 * UNITS, CW), rows_of(chunk, 0, 8 * i, 8), ((1,), (1,)))
            dn = dot(w[u, 2, :, cols], rows_of(chunk, 1, 8 * i, 8), ((1,), (1,)))
            if chunk == 0:
                pre[i, u, : 2 * UNITS], pre[i, u, 2 * UNITS :] = gu, dn
            else:
                pre[i, u, : 2 * UNITS] += gu
                pre[i, u, 2 * UNITS :] += dn

    def begin(i):
        partial(i, 1 - core)
        swap = send(pre.at[i, 1 - core], pre_sib.at[i], t_ss.at[i], t_rs.at[i], sibling)
        partial(i, core)
        return swap

    def pair_up(i, swap):
        swap.wait_recv()
        pre_sib[i] = pre_sib[i] + pre[i, core]
        pre_send[i] = pre_sib[i].astype(BF16)
        return send(pre_send.at[i], pre_recv.at[i], x_ss.at[i], x_rs.at[i], partner)

    def finish(i, copy):
        copy.wait_recv()
        parts = [slice(j * UNITS, (j + 1) * UNITS) for j in range(3)]
        gate_act, up_act, hid_grad = [pre_sib[i, part] + pre_recv[i, part].astype(F32) for part in parts]
        sigmoid_gate = jax.nn.sigmoid(gate_act)
        silu_gate = gate_act * sigmoid_gate
        here = slice(i * ROWS // 2, (i + 1) * ROWS // 2)
        gate_grad = hid_grad * up_act * sigmoid_gate * (1.0 + gate_act * (1.0 - sigmoid_gate))
        act[core, parts[0], here] = gate_grad.astype(BF16)
        act[core, parts[1], here] = (hid_grad * silu_gate).astype(BF16)
        act[core, parts[2], here] = (silu_gate * up_act).astype(BF16)

    for (e, _), crossing in crossings.items():
        if e < 4:
            crossing.wait_recv()
    early = pair_up(0, begin(0))
    for (e, _), crossing in crossings.items():
        if e >= 4:
            crossing.wait_recv()
    swap = begin(1)
    finish(0, early)
    finish(1, pair_up(1, swap))
    swap = send(act.at[core], act.at[core], a_ss, a_rs, sibling)

    def input_part(u):
        act_t[...] = act[u, : 2 * UNITS].astype(F32).T.astype(BF16)
        for chunk in range(NC):
            cols = slice(chunk * CW, (chunk + 1) * CW)
            yield chunk, dot(act_t[...], w[u, :2, :, cols].reshape(2 * UNITS, CW), ((1,), (0,)))

    for chunk, part in input_part(core):
        mine[chunk] = part
    swap.wait_recv()
    for chunk, part in input_part(1 - core):
        mine[chunk] += part

    def own_part(slot, n):
        here = slice(POS[slot] * 16, POS[slot] * 16 + 16)
        per = NC // NB
        parts = [mine[c, here, :] for c in range(n * per, (n + 1) * per)]
        return parts[0] if per == 1 else jnp.concatenate(parts, axis=1)

    outs = []

    def weight_chunk(k, chunk):
        u = 1 - core if k == 0 else core
        cols = slice(chunk * CW, (chunk + 1) * CW)
        there = pl.ds(pl.multiple_of(core * HALF + chunk * CW, CW), CW)
        gu = dot(act[u, : 2 * UNITS], rows_of(chunk, 0), ((1,), (0,))).astype(BF16)
        og[k, 0, :, cols], og[k, 1, :, cols] = gu[:UNITS], gu[UNITS:]
        og[k, 2, :, cols] = dot(act[u, 2 * UNITS :], rows_of(chunk, 1), ((1,), (0,))).astype(BF16)
        for j, ref in enumerate((gate_out, up_out, down_out)):
            src, dst = og.at[k, j, :, cols], ref.at[:, there]
            if k == 0:
                outs.append(send(src, dst, o_ss.at[chunk, j], o_rs.at[chunk, j], sibling))
            else:
                copy = pltpu.make_async_copy(src, dst, o_sem.at[chunk, j])
                copy.start()
                outs.append(copy)

    sums = {}

    def collected(d, dist, n):
        value = own_part((dist if d == 0 else -dist) % NZ, n)
        for child in CHILDREN(dist, RS_J):
            if (d, child, n) in sums:
                sums[d, child, n].wait_recv()
                value = value + rs_recv[d, child - 1, n].astype(F32)
        return value

    before = len(sent)
    for e, dist in enumerate(RS_ORDER):
        for n in range(NB):
            for d in range(2):
                if dist == 8 and (n >= NB // 2) != (d == 1):
                    continue
                rs_send[d, dist - 1, n] = collected(d, dist, n).astype(BF16)
                step = dist - PARENT(dist, RS_J)
                sums[d, dist, n] = send(
                    rs_send.at[d, dist - 1, n], rs_recv.at[d, dist - 1, n],
                    r_ss.at[d, dist - 1, n], r_rs.at[d, dist - 1, n], z_at(step if d == 0 else -step),
                )
        weight_chunk(e // NC, e % NC)
        drain(before * (e + 1) // 8)
    for n in range(NB):
        value = own_part(0, n)
        for d in range(2):
            for child in CHILDREN(0, RS_J):
                sums[d, child, n].wait_recv()
                value = value + rs_recv[d, child - 1, n].astype(F32)
        for s in range(16 // NB):
            fin[:, n * (16 // NB) + s, :] = value[:, s * 128 : (s + 1) * 128]

    last = [
        send(fin.at[spots[k]], fin_recv.at[k], f_ss.at[k], f_rs.at[k], at(z, spots[k])) for k in range(1, NPLANE)
    ]
    drain(len(sent) - len(last))
    for i, copy in enumerate(outs):
        if i < len(outs) // 2:
            copy.wait_recv()
        else:
            copy.wait()
    halves = [fin[pl.ds(me, 1)].reshape(16, 128), None]
    for k in range(1, NPLANE):
        last[k - 1].wait_recv()
        halves[k % 2] = fin_recv[k] if halves[k % 2] is None else halves[k % 2] + fin_recv[k]
    for i, value in enumerate(halves):
        h = core if i == 0 else 1 - core
        for s in range(16):
            line[0:1, pl.ds(pl.multiple_of(h * HALF + s * 128, 128), 128)] = value[s : s + 1, :]
    in_out[...] = line[...].astype(BF16)
    drain(len(sent))


def publish(*refs):
    for src, dst in zip(refs[:4], refs[4:]):
        dst[...] = src[...]


def local(tokens, out_cot, gate_rows, up_rows, down_rows):
    vmem, hbm = pl.BlockSpec(memory_space=pltpu.VMEM), pl.BlockSpec(memory_space=pl.ANY)
    dma = pltpu.SemaphoreType.DMA
    grads = jax.ShapeDtypeStruct((UNITS, WIDTH), BF16)
    shapes = (jax.ShapeDtypeStruct((1, WIDTH), BF16), grads, grads, grads)
    results = pl.pallas_call(
        kernel,
        out_shape=shapes,
        in_specs=[hbm] * 5,
        out_specs=(vmem, hbm, hbm, hbm),
        scratch_shapes=[
            pltpu.VMEM((1, WIDTH), BF16),
            pltpu.VMEM((1, WIDTH), BF16),
            pltpu.VMEM((2, 32, 128), F32),
            pltpu.VMEM((2, 2, 16, 128), BF16),
            pltpu.VMEM((NPLANE, 2, 16, 128), BF16),
            pltpu.VMEM((2, NPLANE, 16, 128), F32),
            pltpu.VMEM((NZ, 16, 2, NPLANE, 128), BF16),
            pltpu.VMEM((2, 3, UNITS, HALF), BF16),
            pltpu.VMEM((2, 2, 3 * UNITS, ROWS // 2), F32),
            pltpu.VMEM((2, 3 * UNITS, ROWS // 2), F32),
            pltpu.VMEM((2, 3 * UNITS, ROWS // 2), BF16),
            pltpu.VMEM((2, 3 * UNITS, ROWS // 2), BF16),
            pltpu.VMEM((2, 3 * UNITS, ROWS), BF16),
            pltpu.VMEM((ROWS, 2 * UNITS), BF16),
            pltpu.VMEM((NC, ROWS, CW), F32),
            pltpu.VMEM((2, 8, NB, 16, HALF // NB), BF16),
            pltpu.VMEM((2, 8, NB, 16, HALF // NB), BF16),
            pltpu.VMEM((NPLANE, 16, 128), F32),
            pltpu.VMEM((NPLANE, 16, 128), F32),
            pltpu.VMEM((1, WIDTH), F32),
            pltpu.VMEM((2, 3, UNITS, HALF), BF16),
            dma((2,)), dma((3,)), dma((3,)), dma((3,)),
            dma((NPLANE,)), dma((NPLANE,)),
            dma((2, 8, 2)), dma((2, 8, 2)),
            dma((8, 4)), dma((8, 4)),
            dma((2,)), dma((2,)),
            dma((2,)), dma((2,)),
            dma, dma,
            dma((2, 8, NB)), dma((2, 8, NB)),
            dma((NPLANE,)), dma((NPLANE,)),
            dma((NC, 3)), dma((NC, 3)), dma((NC, 3)),
        ],
        compiler_params=pltpu.CompilerParams(
            collective_id=0, has_side_effects=True, vmem_limit_bytes=60 * 1024 * 1024
        ),
        name="swiglu_backward",
    )(tokens, out_cot, gate_rows, up_rows, down_rows)
    line = pl.BlockSpec((1, WIDTH), lambda i: (0, 0))
    rows = pl.BlockSpec((UNITS // PARTS, WIDTH), lambda i: (i, 0))
    return pl.pallas_call(
        publish,
        out_shape=shapes,
        grid=(PARTS,),
        in_specs=[line, rows, rows, rows],
        out_specs=(line, rows, rows, rows),
        compiler_params=pltpu.CompilerParams(vmem_limit_bytes=60 * 1024 * 1024),
        name="publish",
    )(*results)


def solution(mesh):
    specs = (P("blk", "pair"),) * 5
    return jax.shard_map(local, mesh=mesh, in_specs=specs, out_specs=specs[:4], check_vma=False)
```
